256 devices in a mesh: dp: 16 (over z, core), tile: 16 (over x, y).
Axes of the slice: x: 4, y: 4, z: 8, core: 2. Of those that a mesh axis runs over, the one named last changes fastest.
Arguments:
- features: bfloat16 [16, 1024, 512], P('dp', 'tile'), may hold values from -6 to 6
- depth_probs: float32 [16, 1024, 118], P('dp', 'tile'), may hold values from 0 to 1, as said below
- context: bfloat16 [16, 1024, 80], P('dp', 'tile'), may hold values from -2 to 2
- bev_grad: bfloat16 [16, 40960, 80], P('dp', 'tile'), may hold values from -18 to 18
- head_weight: bfloat16 [198, 512], replicated, may hold values from -0.4375 to 0.4375
- slot_cell: int32 [16, 16, 16, 512], P('dp', 'tile'), may hold values from 0 to 2559, as said below
- slot_point: int32 [16, 16, 16, 512], P('dp', 'tile'), may hold values from 0 to 7551, as said below
- slot_count: int32 [16, 16, 16], P('dp'), may hold values from 1 to 512, as said below
Outputs:
- grad_features: bfloat16 [16, 1024, 512], P('dp', 'tile')
- head_weight_grad: float32 [512, 198], P('tile')
The draws below stay inside these ranges and needn't reach their ends.
Inputs may be any that keep to these rules, and one draw needn't show every extreme that they name: `slot_count`: every block holds at most 512 live slots; in every scene group one tile receives exactly 512 from every device; the live slots of one device and group sum to at most 7552. `slot_point`: A live slot names a point of the sending device; within one group and sending device each point is named by at most one live slot; dead slots hold 0. `slot_cell`: A live slot names a cell of the receiving tile; dead slots hold 0. `depth_probs`: each pixel's 118 entries are positive and sum to one.
All inputs are finite; a program needn't handle non-finite values.
Results may differ from the reference program's by a relative error of at most 0.0049.
Values may be sent and summed in bfloat16 or wider, within the bound.
No kernel may reach another device: no remote copies, remote signals or barrier semaphores. Data moves between devices by JAX's collectives and lax.ppermute only.
A program may use at most 64 MiB of HBM per device.

```python
import jax
import jax.numpy as jnp
from jax import lax

C = 80
DB = 118
FEAT = 512
PIX_DEV = 64
CELLS_DEV = 2560
CAP = 512
GROUPS = 16
TILES = 16
PIXELS = 1024
BEV_CELLS = 40960
HEAD = 198


def table_counts(key):
    base_key = jax.random.fold_in(key, 11)
    hot_tile = jax.random.randint(jax.random.fold_in(base_key, 1), (GROUPS,), 0, TILES)
    spread = jax.random.randint(jax.random.fold_in(base_key, 2), (GROUPS, TILES, TILES), CAP // 4, CAP // 2 + 1)
    dest_ids = jnp.arange(TILES, dtype=jnp.int32)
    return jnp.where(dest_ids[None, None, :] == hot_tile[:, None, None], CAP, spread).astype(jnp.int32)


def draw_slot_count(key, part):
    return table_counts(key)


def shuffle_one(perm_key):
    return jax.random.permutation(perm_key, PIX_DEV * DB).astype(jnp.int32)


def draw_slot_point(key, part):
    counts = table_counts(key)
    point_total = PIX_DEV * DB
    perm_keys = jax.random.split(jax.random.fold_in(key, 23), GROUPS * TILES)
    shuffled = jax.vmap(shuffle_one)(perm_keys).reshape(GROUPS, TILES, point_total)
    offsets = jnp.cumsum(counts, axis=-1) - counts
    slot_ids = jnp.arange(CAP, dtype=jnp.int32)
    position = jnp.minimum(offsets[..., None] + slot_ids, point_total - 1).astype(jnp.int32)
    picked = jnp.take_along_axis(shuffled, position.reshape(GROUPS, TILES, TILES * CAP), axis=-1)
    picked = picked.reshape(GROUPS, TILES, TILES, CAP)
    return jnp.where(slot_ids < counts[..., None], picked, 0).astype(jnp.int32)


def draw_slot_cell(key, part):
    counts = table_counts(key)
    cells = jax.random.randint(jax.random.fold_in(key, 37), (GROUPS, TILES, TILES, CAP), 0, CELLS_DEV)
    slot_ids = jnp.arange(CAP, dtype=jnp.int32)
    cells = jnp.where(slot_ids < counts[..., None], cells, 0)
    return jnp.transpose(cells, (0, 2, 1, 3)).astype(jnp.int32)


def draw_depth_probs(key, part):
    logits = 0.3 * jax.random.normal(key, (GROUPS, PIXELS, DB), jnp.float32)
    return jax.nn.softmax(logits, axis=-1).astype(jnp.float32)


def spiked(result, rng, source, target, shards_of, factor):
    def block_of(dim):
        return (jnp.arange(result.shape[dim]) // (result.shape[dim] // shards_of)).reshape((-1,) + (1,) * (result.ndim - 1 - dim))

    one_side = jax.random.permutation(rng, shards_of)[block_of(target)]
    second = (block_of(target) + shards_of // 2) % shards_of
    return jnp.where((block_of(source) == one_side) | (block_of(source) == second), factor * result, result)


def block_scale(stream_key, extent, pieces, smallest, high):
    loudness, own = 1.0, jax.random.fold_in(stream_key, 6)
    for axis_at, shards_of in pieces:
        steps = jnp.exp(jax.random.uniform(jax.random.fold_in(own, axis_at), (shards_of,), jnp.float32, smallest / len(pieces), high / len(pieces)))
        loudness = loudness * jnp.repeat(steps, extent[axis_at] // shards_of).reshape([-1 if axis == axis_at else 1 for axis in range(len(extent))])
    return loudness


def normal_values(own_key, dims, scale, most, cuts=(), kind=jnp.bfloat16):
    gain = block_scale(own_key, dims, cuts, -0.22, 0.18) if cuts else 1.0
    result = jax.random.normal(own_key, dims, jnp.float32) * scale * gain
    return jnp.minimum(jnp.maximum(result, -most), most).astype(kind)


def noise_with(rng, dims, scale, bound, cuts, heavy, kind=jnp.bfloat16):
    drawn = scale * jax.random.normal(rng, dims, jnp.float32)
    if cuts:
        drawn = drawn * block_scale(rng, dims, cuts, -0.22, 0.18)
    return jnp.clip(spiked(drawn, jax.random.fold_in(rng, 3), *heavy), -bound, bound).astype(kind)


def setup_inputs(seed: int = 0) -> dict:
    splits = jax.random.split(jax.random.key(seed), 9)
    return {
        "features": noise_with(splits[0], (GROUPS, PIXELS, FEAT), 1.0, 6.0, ((0, 16), (1, 16)), (1, 2, 16, 2.0)),
        "depth_probs": draw_depth_probs(jax.random.fold_in(splits[8], 71), 0),
        "context": normal_values(splits[2], (GROUPS, PIXELS, C), 0.3, 2.0, ((0, 16), (1, 16))),
        "bev_grad": normal_values(splits[3], (GROUPS, BEV_CELLS, C), 3.0, 18.0, ((0, 16), (1, 16))),
        "head_weight": normal_values(splits[4], (HEAD, FEAT), HEAD ** -0.5, 0.4375),
        "slot_cell": draw_slot_cell(jax.random.fold_in(splits[8], 71), 0),
        "slot_point": draw_slot_point(jax.random.fold_in(splits[8], 71), 0),
        "slot_count": draw_slot_count(jax.random.fold_in(splits[8], 71), 0),
    }


def one_group(features, depth_probs, context, bev_grad, slot_cell, slot_point, slot_count, head_weight):
    tile_count = slot_count.shape[0]
    cell_by_src = jnp.transpose(slot_cell, (1, 0, 2))
    tile_ids = jnp.arange(tile_count, dtype=jnp.int32)
    global_cell = cell_by_src + (tile_ids * CELLS_DEV).astype(jnp.int32)[None, :, None]
    global_point = slot_point + (tile_ids * (PIX_DEV * DB)).astype(jnp.int32)[:, None, None]
    live_slots = jnp.arange(CAP, dtype=jnp.int32)[None, None, :] < slot_count[:, :, None]
    looked_up = bev_grad[global_cell.reshape(-1)].reshape(tile_count, tile_count, CAP, C)
    looked_up = jnp.where(live_slots[..., None], looked_up, jnp.zeros((), bev_grad.dtype))
    point_grads = jnp.zeros((tile_count * PIX_DEV * DB, C), bev_grad.dtype)
    point_grads = point_grads.at[global_point.reshape(-1)].add(looked_up.reshape(-1, C))
    point_grads = point_grads.reshape(tile_count * PIX_DEV, DB, C).astype(jnp.float32)
    context32 = context.astype(jnp.float32)
    grad_depth = jnp.einsum('pdc,pc->pd', point_grads, context32, precision=lax.Precision.HIGHEST)
    grad_ctx = jnp.einsum('pd,pdc->pc', depth_probs, point_grads, precision=lax.Precision.HIGHEST)
    grad_logits = depth_probs * (grad_depth - jnp.sum(depth_probs * grad_depth, axis=-1, keepdims=True))
    head_grad = jnp.concatenate([grad_logits, grad_ctx], axis=-1).astype(jnp.bfloat16)
    grad_feats = jnp.dot(head_grad, head_weight, preferred_element_type=jnp.float32).astype(jnp.bfloat16)
    weight_term = jnp.dot(features.T, head_grad, preferred_element_type=jnp.float32)
    return grad_feats, weight_term


def reference(features, depth_probs, context, bev_grad, head_weight, slot_cell, slot_point, slot_count):
    def accumulate(summed, group_items):
        grad_feats, weight_term = one_group(*group_items, head_weight)
        return summed + weight_term, grad_feats

    initial = jnp.zeros((FEAT, DB + C), jnp.float32)
    summed, grad_feats = lax.scan(accumulate, initial, (features, depth_probs, context, bev_grad, slot_cell, slot_point, slot_count))
    return grad_feats, summed
```

```python
import jax
import jax.numpy as jnp
from jax import lax
from jax.experimental import pallas as pl
from jax.experimental.pallas import tpu as pltpu
from jax.sharding import Mesh, PartitionSpec as P

F32, BF16 = jnp.float32, jnp.bfloat16
LOW = 512
HALF = 256
NT = (((1,), (1,)), ((), ()))
TN = (((0,), (0,)), ((), ()))
VMEM = pl.BlockSpec(memory_space=pltpu.VMEM)
SMEM = pl.BlockSpec(memory_space=pltpu.SMEM)


def row_hot(index_row, rows, value):
    ids = lax.broadcasted_iota(jnp.int32, (rows, index_row.shape[1]), 0).astype(F32).astype(BF16)
    return jnp.where(ids == index_row, value, jnp.zeros((), BF16))


def lookup_kernel(tile_ref, counts_ref, bev_ref, cells_ref, out_ref, table_ref):
    cells_dev, channels = bev_ref.shape
    blocks = cells_dev // LOW
    capacity = cells_ref.shape[1]
    tile = tile_ref[0]
    for j in range(blocks):
        table_ref[pl.ds(j * channels, channels), :] = bev_ref[pl.ds(j * LOW, LOW), :].T
    slot = lax.broadcasted_iota(jnp.int32, (1, capacity), 1)
    for s in range(cells_ref.shape[0]):
        cell = cells_ref[pl.ds(s, 1), :]
        live = slot < counts_ref[s, tile]
        low = cell & (HALF - 1)
        hots = []
        for h in range(LOW // HALF):
            here = live & (((cell >> 8) & (LOW // HALF - 1)) == h)
            index = jnp.where(here, low, -1).astype(F32).astype(BF16)
            hots.append(row_hot(index, HALF, jnp.ones((), BF16)))
        picked = jnp.dot(
            table_ref[...], jnp.concatenate(hots, axis=0), preferred_element_type=F32
        )
        block = cell >> 9
        found = picked[:channels]
        for j in range(1, blocks):
            found = jnp.where(block == j, picked[j * channels : (j + 1) * channels], found)
        out_ref[s] = found.astype(BF16)


def lookup(tile, counts, bev_rows, cells):
    sources, capacity = cells.shape
    cells_dev, channels = bev_rows.shape
    return pl.pallas_call(
        lookup_kernel,
        out_shape=jax.ShapeDtypeStruct((sources, channels, capacity), BF16),
        in_specs=[SMEM, SMEM, VMEM, VMEM],
        out_specs=VMEM,
        scratch_shapes=[pltpu.VMEM((cells_dev // LOW * channels, LOW), BF16)],
        compiler_params=pltpu.CompilerParams(vmem_limit_bytes=40 * 2**20),
        cost_estimate=pl.CostEstimate(flops=8 * 10**9, bytes_accessed=4 * 10**6, transcendentals=0),
        name="lookup",
    )(tile, counts, bev_rows, cells)


def halves(value):
    high = value.astype(BF16)
    return high, (value - high.astype(F32)).astype(BF16)


def split_points(points, depth_bins):
    pixel = (points.astype(F32) + 0.5) * (1.0 / depth_bins)
    pixel = pixel.astype(jnp.int32)
    return pixel, points - pixel * depth_bins


def as_index(value):
    return value.astype(F32).astype(BF16)


def slots_kernel(points_ref, probs_ref, context_ref, pixel_ref, bin_ref, prob_ref, ctx_ref):
    pixels, depth_bins = probs_ref.shape
    channels = context_ref.shape[1]
    probs_high, probs_low = halves(probs_ref[...])
    pad = jnp.zeros((pixels, 128 - depth_bins), BF16)
    table = jnp.concatenate(
        [probs_high, pad, probs_low, pad, context_ref[...]], axis=1
    )
    for s in range(points_ref.shape[0]):
        pixel, bins = split_points(points_ref[pl.ds(s, 1), :], depth_bins)
        hot = row_hot(as_index(pixel), pixels, jnp.ones((), BF16))
        spread = lax.dot_general(table, hot, TN, preferred_element_type=F32)
        both = spread[:128] + spread[128:256]
        ids = lax.broadcasted_iota(jnp.int32, both.shape, 0)
        prob_ref[pl.ds(s, 1), :] = jnp.sum(jnp.where(ids == bins, both, 0.0), axis=0, keepdims=True)
        ctx_ref[s] = spread[256 : 256 + channels].astype(BF16)
        pixel_ref[pl.ds(s, 1), :] = pixel
        bin_ref[pl.ds(s, 1), :] = bins


def slots(points, depth_probs, context):
    sources, capacity = points.shape
    channels = context.shape[1]
    row = (sources, capacity)
    return pl.pallas_call(
        slots_kernel,
        out_shape=[
            jax.ShapeDtypeStruct(row, jnp.int32),
            jax.ShapeDtypeStruct(row, jnp.int32),
            jax.ShapeDtypeStruct(row, F32),
            jax.ShapeDtypeStruct((sources, channels, capacity), BF16),
        ],
        in_specs=[VMEM] * 3,
        out_specs=[VMEM] * 4,
        compiler_params=pltpu.CompilerParams(vmem_limit_bytes=40 * 2**20),
        cost_estimate=pl.CostEstimate(flops=4 * 10**9, bytes_accessed=3 * 10**6, transcendentals=0),
        name="slots",
    )(points, depth_probs, context)


def head_kernel(
    arrived_ref, pixel_ref, bin_ref, prob_ref, ctx_ref, probs_ref, features_ref, grad_ref, weight_ref
):
    pixels, depth_bins = probs_ref.shape
    sources, channels, capacity = arrived_ref.shape
    total = jnp.zeros((4 * pixels, 128 + channels), F32)
    for s in range(sources):
        arrived = arrived_ref[s]
        slot_grad = jnp.sum(
            arrived.astype(F32) * ctx_ref[s].astype(F32), axis=0, keepdims=True
        )
        pixel = as_index(pixel_ref[pl.ds(s, 1), :])
        bins = as_index(bin_ref[pl.ds(s, 1), :])
        weights = [*halves(slot_grad), *halves(prob_ref[pl.ds(s, 1), :])]
        left = jnp.concatenate([row_hot(pixel, pixels, weight) for weight in weights], axis=0)
        right = jnp.concatenate([row_hot(bins, 128, jnp.ones((), BF16)), arrived], axis=0)
        total += lax.dot_general(left, right, NT, preferred_element_type=F32)
    grad_depth = (total[:pixels] + total[pixels : 2 * pixels])[:, :depth_bins]
    grad_ctx = (total[2 * pixels : 3 * pixels] + total[3 * pixels :])[:, 128:]
    probs = probs_ref[...]
    grad_logits = probs * (grad_depth - jnp.sum(probs * grad_depth, axis=-1, keepdims=True))
    head_grad = jnp.concatenate([grad_logits, grad_ctx], axis=-1).astype(BF16)
    grad_ref[...] = head_grad
    weight_ref[...] = lax.dot_general(features_ref[...], head_grad, TN, preferred_element_type=F32)


def head(arrived, pixel, bins, prob, ctx, depth_probs, features):
    pixels, depth_bins = depth_probs.shape
    channels = arrived.shape[1]
    return pl.pallas_call(
        head_kernel,
        out_shape=[
            jax.ShapeDtypeStruct((pixels, depth_bins + channels), BF16),
            jax.ShapeDtypeStruct((features.shape[1], depth_bins + channels), F32),
        ],
        in_specs=[VMEM] * 7,
        out_specs=[VMEM] * 2,
        compiler_params=pltpu.CompilerParams(vmem_limit_bytes=40 * 2**20),
        cost_estimate=pl.CostEstimate(flops=4 * 10**9, bytes_accessed=4 * 10**6, transcendentals=0),
        name="head",
    )(arrived, pixel, bins, prob, ctx, depth_probs, features)


def exchange(value, axis):
    return lax.all_to_all(value, axis, split_axis=0, concat_axis=0, tiled=True)


def body(features, depth_probs, context, bev_grad, head_weight, slot_cell, slot_point, slot_count):
    tiles = lax.axis_size(("x", "y"))
    tile = lax.axis_index(("x", "y")).astype(jnp.int32).reshape(1)
    found = lookup(tile, slot_count[0], bev_grad[0], slot_cell[0, 0])
    pixel, bins, prob, ctx = slots(slot_point[0, 0], depth_probs[0], context[0])
    arrived = exchange(found, ("x", "y"))
    head_grad, weight_grad = head(
        arrived, pixel, bins, prob, ctx, depth_probs[0], features[0]
    )
    rows = weight_grad.shape[0] // tiles
    share = exchange(weight_grad.reshape(tiles, rows, -1), ("x", "y")).sum(axis=0)
    grad_feats = jnp.dot(head_grad, head_weight, preferred_element_type=F32).astype(BF16)
    cores = lax.axis_size("core")
    other = lax.ppermute(share, "core", [(i, (i + 1) % cores) for i in range(cores)])
    share = share + other
    everyone = jnp.broadcast_to(share[None], (lax.axis_size("z"),) + share.shape)
    summed = exchange(everyone, "z").sum(axis=0)
    return (grad_feats[None], summed)


def solution(mesh):
    dp, tile = ("z", "core"), ("x", "y")
    fine = Mesh(mesh.devices.reshape(8, 2, 4, 4), dp + tile)
    return jax.shard_map(
        body,
        mesh=fine,
        in_specs=(
            P(dp, tile, None),
            P(dp, tile, None),
            P(dp, tile, None),
            P(dp, tile, None),
            P(),
            P(dp, tile, None, None),
            P(dp, tile, None, None),
            P(dp, None, None),
        ),
        out_specs=(P(dp, tile, None), P(tile, None)),
        check_vma=False,
    )
```

```python
import jax
import jax.numpy as jnp
from jax import lax
from jax.experimental import pallas as pl
from jax.experimental.pallas import tpu as pltpu
from jax.sharding import Mesh, PartitionSpec as P

F32, BF16 = jnp.float32, jnp.bfloat16
LOW = 512
HALF = 256
NT = (((1,), (1,)), ((), ()))
TN = (((0,), (0,)), ((), ()))
VMEM = pl.BlockSpec(memory_space=pltpu.VMEM)
SMEM = pl.BlockSpec(memory_space=pltpu.SMEM)
HBM = pl.BlockSpec(memory_space=pltpu.HBM)


def row_hot(index_row, rows, value):
    ids = lax.broadcasted_iota(jnp.int32, (rows, index_row.shape[1]), 0).astype(F32).astype(BF16)
    return jnp.where(ids == index_row, value, jnp.zeros((), BF16))


def halves(value):
    high = value.astype(BF16)
    return high, (value - high.astype(F32)).astype(BF16)


def split_points(points, depth_bins):
    pixel = (points.astype(F32) + 0.5) * (1.0 / depth_bins)
    pixel = pixel.astype(jnp.int32)
    return pixel, points - pixel * depth_bins


def as_index(value):
    return value.astype(F32).astype(BF16)


def lookup_tables(cell, live):
    low = cell & (HALF - 1)
    hots = []
    for h in range(LOW // HALF):
        here = live & (((cell >> 8) & (LOW // HALF - 1)) == h)
        hots.append(row_hot(as_index(jnp.where(here, low, -1)), HALF, jnp.ones((), BF16)))
    return jnp.concatenate(hots, axis=0), cell >> 9


def front_kernel(
    tile_ref, bev_hbm, cells_hbm, counts_hbm, points_hbm, probs_hbm, context_hbm,
    found_ref, prob_ref, ctx_ref,
    bev_ref, cells_ref, counts_ref, points_ref, probs_ref, context_ref, sems,
):
    channels = context_ref.shape[1]
    blocks = bev_ref.shape[0] // channels
    sources, capacity = cells_ref.shape
    pixels, depth_bins = probs_ref.shape
    copies = [
        pltpu.make_async_copy(source, target, sems.at[i])
        for i, (source, target) in enumerate([
            (counts_hbm, counts_ref),
            (cells_hbm, cells_ref),
            (points_hbm, points_ref),
            (probs_hbm, probs_ref),
            (context_hbm, context_ref),
            *(
                (bev_hbm.at[:, pl.ds(j * LOW, LOW)], bev_ref.at[pl.ds(j * channels, channels), :])
                for j in range(blocks)
            ),
        ])
    ]
    for copy in copies:
        copy.start()
    for copy in copies:
        copy.wait()
    tile = tile_ref[0]
    slot = lax.broadcasted_iota(jnp.int32, (1, capacity), 1)
    probs_high, probs_low = halves(probs_ref[...])
    pad = jnp.zeros((pixels, 128 - depth_bins), BF16)
    table = jnp.concatenate([probs_high, pad, probs_low, pad, context_ref[...]], axis=1).T
    for s in range(sources):
        hot, block = lookup_tables(cells_ref[pl.ds(s, 1), :], slot < counts_ref[s, tile])
        picked = jnp.dot(bev_ref[...], hot, preferred_element_type=F32)
        found = picked[:channels]
        for j in range(1, blocks):
            found = jnp.where(block == j, picked[j * channels : (j + 1) * channels], found)
        found_ref[s] = found.astype(BF16)
        pixel, bins = split_points(points_ref[pl.ds(s, 1), :], depth_bins)
        spread = jnp.dot(
            table, row_hot(as_index(pixel), pixels, jnp.ones((), BF16)), preferred_element_type=F32
        )
        both = spread[:128] + spread[128:256]
        ids = lax.broadcasted_iota(jnp.int32, both.shape, 0)
        prob_ref[pl.ds(s, 1), :] = jnp.sum(jnp.where(ids == bins, both, 0.0), axis=0, keepdims=True)
        ctx_ref[s] = spread[256 : 256 + channels].astype(BF16)


def front(tile, bev_columns, cells, counts, points, depth_probs, context):
    sources, capacity = cells.shape
    channels, cells_dev = bev_columns.shape
    blocks = cells_dev // LOW
    return pl.pallas_call(
        front_kernel,
        out_shape=[
            jax.ShapeDtypeStruct((sources, channels, capacity), BF16),
            jax.ShapeDtypeStruct((sources, capacity), F32),
            jax.ShapeDtypeStruct((sources, channels, capacity), BF16),
        ],
        in_specs=[SMEM] + [HBM] * 6,
        out_specs=[VMEM] * 3,
        scratch_shapes=[
            pltpu.VMEM((blocks * channels, LOW), BF16),
            pltpu.VMEM(cells.shape, jnp.int32),
            pltpu.SMEM(counts.shape, jnp.int32),
            pltpu.VMEM(points.shape, jnp.int32),
            pltpu.VMEM(depth_probs.shape, F32),
            pltpu.VMEM(context.shape, BF16),
            pltpu.SemaphoreType.DMA((5 + blocks,)),
        ],
        compiler_params=pltpu.CompilerParams(vmem_limit_bytes=40 * 2**20),
        cost_estimate=pl.CostEstimate(flops=8 * 10**9, bytes_accessed=4 * 10**6, transcendentals=0),
        name="front",
    )(tile, *(
        pltpu.with_memory_space_constraint(value, pltpu.HBM)
        for value in (bev_columns, cells, counts, points, depth_probs, context)
    ))


def head_kernel(
    arrived_ref, points_ref, prob_ref, ctx_ref, probs_ref, features_ref, grad_ref, weight_ref
):
    pixels, depth_bins = probs_ref.shape
    sources, channels, capacity = arrived_ref.shape
    total = jnp.zeros((4 * pixels, 128 + channels), F32)
    for s in range(sources):
        arrived = arrived_ref[s]
        slot_grad = jnp.sum(
            arrived.astype(F32) * ctx_ref[s].astype(F32), axis=0, keepdims=True
        )
        pixel, bins = map(as_index, split_points(points_ref[pl.ds(s, 1), :], depth_bins))
        weights = [*halves(slot_grad), *halves(prob_ref[pl.ds(s, 1), :])]
        left = jnp.concatenate([row_hot(pixel, pixels, weight) for weight in weights], axis=0)
        right = jnp.concatenate([row_hot(bins, 128, jnp.ones((), BF16)), arrived], axis=0)
        total += lax.dot_general(left, right, NT, preferred_element_type=F32)
    grad_depth = (total[:pixels] + total[pixels : 2 * pixels])[:, :depth_bins]
    grad_ctx = (total[2 * pixels : 3 * pixels] + total[3 * pixels :])[:, 128:]
    probs = probs_ref[...]
    grad_logits = probs * (grad_depth - jnp.sum(probs * grad_depth, axis=-1, keepdims=True))
    head_grad = jnp.concatenate([grad_logits, grad_ctx], axis=-1).astype(BF16)
    grad_ref[...] = head_grad
    weight_ref[...] = lax.dot_general(features_ref[...], head_grad, TN, preferred_element_type=F32)


def head(arrived, points, prob, ctx, depth_probs, features):
    pixels, depth_bins = depth_probs.shape
    channels = arrived.shape[1]
    return pl.pallas_call(
        head_kernel,
        out_shape=[
            jax.ShapeDtypeStruct((pixels, depth_bins + channels), BF16),
            jax.ShapeDtypeStruct((features.shape[1], depth_bins + channels), F32),
        ],
        in_specs=[VMEM] * 6,
        out_specs=[VMEM] * 2,
        compiler_params=pltpu.CompilerParams(vmem_limit_bytes=40 * 2**20),
        cost_estimate=pl.CostEstimate(flops=4 * 10**9, bytes_accessed=4 * 10**6, transcendentals=0),
        name="head",
    )(arrived, points, prob, ctx, depth_probs, features)


def exchange(value, axis):
    return lax.all_to_all(value, axis, split_axis=0, concat_axis=0, tiled=True)


def moved(value, axis, distance):
    size = lax.axis_size(axis)
    return lax.ppermute(value, axis, [(i, (i + distance) % size) for i in range(size)])


def swapped(value, axis, bit):
    return lax.ppermute(value, axis, [(i, i ^ bit) for i in range(lax.axis_size(axis))])


def sum_over_groups(share):
    share = share + swapped(share, "core", 1)
    share = share + swapped(share, "z", 1)
    across = moved(share, "z", 4)
    ahead, behind = moved(share, "z", 2), moved(share, "z", -2)
    return (share + across) + (ahead + behind)


def body(features, depth_probs, context, bev_grad, head_weight, slot_cell, slot_point, slot_count):
    tile_axes = ("x", "y")
    tiles = lax.axis_size(tile_axes)
    tile = lax.axis_index(tile_axes).astype(jnp.int32).reshape(1)
    points = slot_point[0, 0]
    found, prob, ctx = front(
        tile, bev_grad[0].T, slot_cell[0, 0], slot_count[0], points, depth_probs[0], context[0]
    )
    arrived = exchange(found, tile_axes)
    head_grad, weight_grad = head(arrived, points, prob, ctx, depth_probs[0], features[0])
    rows = weight_grad.shape[0] // tiles
    share = exchange(weight_grad.reshape(tiles, rows, -1), tile_axes).sum(axis=0)
    grad_feats = jnp.dot(head_grad, head_weight, preferred_element_type=F32).astype(BF16)
    return (grad_feats[None], sum_over_groups(share))


def solution(mesh):
    dp, tile = ("z", "core"), ("x", "y")
    fine = Mesh(mesh.devices.reshape(8, 2, 4, 4), dp + tile)
    return jax.shard_map(
        body,
        mesh=fine,
        in_specs=(
            P(dp, tile, None),
            P(dp, tile, None),
            P(dp, tile, None),
            P(dp, tile, None),
            P(),
            P(dp, tile, None, None),
            P(dp, tile, None, None),
            P(dp, None, None),
        ),
        out_specs=(P(dp, tile, None), P(tile, None)),
        check_vma=False,
    )
```

```python
import jax
import jax.numpy as jnp
from jax import lax
from jax.experimental import pallas as pl
from jax.experimental.pallas import tpu as pltpu
from jax.sharding import Mesh, PartitionSpec as P

F32, BF16 = jnp.float32, jnp.bfloat16
LOW = 512
LANES = 128
HALF = 256
NT = (((1,), (1,)), ((), ()))
TN = (((0,), (0,)), ((), ()))
VMEM = pl.BlockSpec(memory_space=pltpu.VMEM)
SMEM = pl.BlockSpec(memory_space=pltpu.SMEM)
HBM = pl.BlockSpec(memory_space=pltpu.HBM)


def row_ids(rows):
    return lax.broadcasted_iota(jnp.int32, (rows, LANES), 0)


def as_index(value):
    return value.astype(F32).astype(BF16)


def by_lanes(make, columns):
    return jnp.concatenate([make(slice(i, i + LANES)) for i in range(0, columns, LANES)], axis=1)


def row_hot(ids, index_row, value_row):
    zero = jnp.zeros((), value_row.dtype)
    return by_lanes(
        lambda at: jnp.where(ids == index_row[:, at], value_row[:, at], zero), index_row.shape[1]
    )


def halves(value):
    high = value.astype(BF16)
    return high, (value - high.astype(F32)).astype(BF16)


def split_points(points, depth_bins):
    pixel = (points.astype(F32) + 0.5) * (1.0 / depth_bins)
    pixel = pixel.astype(jnp.int32)
    return pixel, points - pixel * depth_bins


def lookup_tables(ids, ones, cell, live):
    low = cell & (HALF - 1)
    hots = []
    for h in range(LOW // HALF):
        here = live & (((cell >> 8) & (LOW // HALF - 1)) == h)
        hots.append(row_hot(ids, as_index(jnp.where(here, low, -1)), ones))
    return jnp.concatenate(hots, axis=0), cell >> (LOW.bit_length() - 1)


def front_kernel(
    tile_ref, bev_hbm, cells_hbm, counts_hbm, points_hbm, probs_hbm, context_hbm,
    found_ref, prob_ref, ctx_ref,
    bev_ref, cells_ref, counts_ref, points_ref, probs_ref, context_ref, sems,
):
    channels = context_ref.shape[1]
    blocks = bev_ref.shape[0] // channels
    sources, capacity = cells_ref.shape
    pixels, depth_bins = probs_ref.shape
    copies = [
        pltpu.make_async_copy(source, target, sems.at[i])
        for i, (source, target) in enumerate([
            (counts_hbm, counts_ref),
            (cells_hbm, cells_ref),
            (points_hbm, points_ref),
            (probs_hbm, probs_ref),
            (context_hbm, context_ref),
            *(
                (bev_hbm.at[:, pl.ds(j * LOW, LOW)], bev_ref.at[pl.ds(j * channels, channels), :])
                for j in range(blocks)
            ),
        ])
    ]
    for copy in copies:
        copy.start()
    for copy in copies:
        copy.wait()
    tile = tile_ref[0]
    slot = lax.broadcasted_iota(jnp.int32, (1, capacity), 1)
    ids, ids32 = as_index(row_ids(HALF)), row_ids(LANES)
    ones = jnp.ones((1, capacity), BF16)
    high, low = (half.T for half in halves(probs_ref[...]))
    pad = jnp.zeros((LANES - depth_bins, 2 * pixels), BF16)
    context = context_ref[...].T
    table = jnp.concatenate(
        [
            jnp.concatenate([high, low], axis=1),
            pad,
            jnp.concatenate([context, jnp.zeros_like(context)], axis=1),
        ],
        axis=0,
    )
    for s in range(sources):
        hot, block = lookup_tables(ids, ones, cells_ref[pl.ds(s, 1), :], slot < counts_ref[s, tile])
        picked = jnp.dot(bev_ref[...], hot, preferred_element_type=F32)
        found = picked[:channels]
        for j in range(1, blocks):
            found = jnp.where(block == j, picked[j * channels : (j + 1) * channels], found)
        found_ref[s] = found.astype(BF16)
        pixel, bins = split_points(points_ref[pl.ds(s, 1), :], depth_bins)
        hot = row_hot(ids[:pixels], as_index(pixel), ones)
        spread = jnp.dot(table, jnp.concatenate([hot, hot], axis=0), preferred_element_type=F32)
        prob_ref[pl.ds(s, 1), :] = by_lanes(
            lambda at: jnp.sum(
                jnp.where(ids32 == bins[:, at], spread[:LANES, at], 0.0), axis=0, keepdims=True
            ),
            capacity,
        )
        ctx_ref[s] = spread[LANES:].astype(BF16)


def front(tile, bev_columns, cells, counts, points, depth_probs, context):
    sources, capacity = cells.shape
    channels, cells_dev = bev_columns.shape
    blocks = cells_dev // LOW
    return pl.pallas_call(
        front_kernel,
        out_shape=[
            jax.ShapeDtypeStruct((sources, channels, capacity), BF16),
            jax.ShapeDtypeStruct((sources, capacity), F32),
            jax.ShapeDtypeStruct((sources, channels, capacity), BF16),
        ],
        in_specs=[SMEM] + [HBM] * 6,
        out_specs=[VMEM] * 3,
        scratch_shapes=[
            pltpu.VMEM((blocks * channels, LOW), BF16),
            pltpu.VMEM(cells.shape, jnp.int32),
            pltpu.SMEM(counts.shape, jnp.int32),
            pltpu.VMEM(points.shape, jnp.int32),
            pltpu.VMEM(depth_probs.shape, F32),
            pltpu.VMEM(context.shape, BF16),
            pltpu.SemaphoreType.DMA((5 + blocks,)),
        ],
        compiler_params=pltpu.CompilerParams(vmem_limit_bytes=40 * 2**20),
        cost_estimate=pl.CostEstimate(flops=8 * 10**9, bytes_accessed=4 * 10**6, transcendentals=0),
        name="front",
    )(tile, *(
        pltpu.with_memory_space_constraint(value, pltpu.HBM)
        for value in (bev_columns, cells, counts, points, depth_probs, context)
    ))


def head_kernel(
    arrived_ref, points_ref, prob_ref, ctx_ref, probs_ref, features_ref, grad_ref, weight_ref
):
    pixels, depth_bins = probs_ref.shape
    sources, channels, capacity = arrived_ref.shape
    ids = as_index(row_ids(LANES))
    ones = jnp.ones((1, capacity), BF16)
    total = jnp.zeros((4 * pixels, LANES + channels), F32)
    for s in range(sources):
        arrived = arrived_ref[s]
        slot_grad = jnp.sum(
            arrived.astype(F32) * ctx_ref[s].astype(F32), axis=0, keepdims=True
        )
        pixel, bins = map(as_index, split_points(points_ref[pl.ds(s, 1), :], depth_bins))
        weights = [*halves(slot_grad), *halves(prob_ref[pl.ds(s, 1), :])]
        left = jnp.concatenate([row_hot(ids[:pixels], pixel, weight) for weight in weights], axis=0)
        right = jnp.concatenate([row_hot(ids, bins, ones), arrived], axis=0)
        total += lax.dot_general(left, right, NT, preferred_element_type=F32)
    grad_depth = (total[:pixels] + total[pixels : 2 * pixels])[:, :depth_bins]
    grad_ctx = (total[2 * pixels : 3 * pixels] + total[3 * pixels :])[:, LANES:]
    probs = probs_ref[...]
    grad_logits = probs * (grad_depth - jnp.sum(probs * grad_depth, axis=-1, keepdims=True))
    head_grad = jnp.concatenate([grad_logits, grad_ctx], axis=-1).astype(BF16)
    grad_ref[...] = head_grad
    weight_ref[...] = lax.dot_general(
        features_ref[...], head_grad, TN, preferred_element_type=F32
    ).astype(BF16)


def head(arrived, points, prob, ctx, depth_probs, features):
    pixels, depth_bins = depth_probs.shape
    channels = arrived.shape[1]
    return pl.pallas_call(
        head_kernel,
        out_shape=[
            jax.ShapeDtypeStruct((pixels, depth_bins + channels), BF16),
            jax.ShapeDtypeStruct((features.shape[1], depth_bins + channels), BF16),
        ],
        in_specs=[VMEM] * 6,
        out_specs=[VMEM] * 2,
        compiler_params=pltpu.CompilerParams(vmem_limit_bytes=40 * 2**20),
        cost_estimate=pl.CostEstimate(flops=4 * 10**9, bytes_accessed=4 * 10**6, transcendentals=0),
        name="head",
    )(arrived, points, prob, ctx, depth_probs, features)


def exchange(value, axis):
    return lax.all_to_all(value, axis, split_axis=0, concat_axis=0, tiled=True)


def moved(value, axis, distance):
    size = lax.axis_size(axis)
    return lax.ppermute(value, axis, [(i, (i + distance) % size) for i in range(size)])


def swapped(value, axis, bit):
    return lax.ppermute(value, axis, [(i, i ^ bit) for i in range(lax.axis_size(axis))])


def sum_over_groups(share):
    share = share + swapped(share, "core", 1)
    share = share + swapped(share, "z", 1)
    ahead, behind = moved(share, "z", 2), moved(share, "z", -2)
    across = moved(share, "z", 4)
    return (ahead + behind) + (share + across)


def body(features, depth_probs, context, bev_grad, head_weight, slot_cell, slot_point, slot_count):
    tile_axes = ("x", "y")
    tiles = lax.axis_size(tile_axes)
    tile = lax.axis_index(tile_axes).astype(jnp.int32).reshape(1)
    points = slot_point[0, 0]
    found, prob, ctx = front(
        tile, bev_grad[0].T, slot_cell[0, 0], slot_count[0], points, depth_probs[0], context[0]
    )
    arrived = exchange(found, tile_axes)
    head_grad, weight_grad = head(arrived, points, prob, ctx, depth_probs[0], features[0])
    rows = weight_grad.shape[0] // tiles
    parts = exchange(weight_grad.reshape(tiles, rows, -1), tile_axes)
    share = parts.astype(F32).sum(axis=0)
    grad_feats = jnp.dot(head_grad, head_weight, preferred_element_type=F32).astype(BF16)
    return (grad_feats[None], sum_over_groups(share))


def solution(mesh):
    dp, tile = ("z", "core"), ("x", "y")
    fine = Mesh(mesh.devices.reshape(8, 2, 4, 4), dp + tile)
    return jax.shard_map(
        body,
        mesh=fine,
        in_specs=(
            P(dp, tile, None),
            P(dp, tile, None),
            P(dp, tile, None),
            P(dp, tile, None),
            P(),
            P(dp, tile, None, None),
            P(dp, tile, None, None),
            P(dp, None, None),
        ),
        out_specs=(P(dp, tile, None), P(tile, None)),
        check_vma=False,
    )
```

```python
import jax
import jax.numpy as jnp
from jax import lax
from jax.experimental import pallas as pl
from jax.experimental.pallas import tpu as pltpu
from jax.sharding import Mesh, PartitionSpec as P

F32, BF16 = jnp.float32, jnp.bfloat16
LOW = 512
LANES = 128
HALF = 256
NT = (((1,), (1,)), ((), ()))
TN = (((0,), (0,)), ((), ()))
VMEM = pl.BlockSpec(memory_space=pltpu.VMEM)
SMEM = pl.BlockSpec(memory_space=pltpu.SMEM)
HBM = pl.BlockSpec(memory_space=pltpu.HBM)


def row_ids(rows):
    return lax.broadcasted_iota(jnp.int32, (rows, LANES), 0)


def as_index(value):
    return value.astype(F32).astype(BF16)


def by_lanes(make, columns):
    return jnp.concatenate([make(slice(i, i + LANES)) for i in range(0, columns, LANES)], axis=1)


def row_hot(ids, index_row, value_row):
    zero = jnp.zeros((), value_row.dtype)
    return by_lanes(
        lambda at: jnp.where(ids == index_row[:, at], value_row[:, at], zero), index_row.shape[1]
    )


def halves(value):
    high = value.astype(BF16)
    return high, (value - high.astype(F32)).astype(BF16)


def split_points(points, depth_bins):
    pixel = (points.astype(F32) + 0.5) * (1.0 / depth_bins)
    pixel = pixel.astype(jnp.int32)
    return pixel, points - pixel * depth_bins


def lookup_tables(ids, ones, cell, live):
    low = cell & (HALF - 1)
    hots = []
    for h in range(LOW // HALF):
        here = live & (((cell >> 8) & (LOW // HALF - 1)) == h)
        hots.append(row_hot(ids, as_index(jnp.where(here, low, -1)), ones))
    return jnp.concatenate(hots, axis=0), cell >> (LOW.bit_length() - 1)


def front_kernel(
    tile_ref, bev_hbm, cells_hbm, counts_hbm, points_hbm, probs_hbm, context_hbm,
    found_ref, prob_ref, ctx_ref,
    bev_ref, cells_ref, counts_ref, points_ref, probs_ref, context_ref, sems,
):
    channels = context_ref.shape[1]
    blocks = bev_ref.shape[0] // channels
    sources, capacity = cells_ref.shape
    pixels, depth_bins = probs_ref.shape
    copies = [
        pltpu.make_async_copy(source, target, sems.at[i])
        for i, (source, target) in enumerate([
            (counts_hbm, counts_ref),
            (cells_hbm, cells_ref),
            (points_hbm, points_ref),
            (probs_hbm, probs_ref),
            (context_hbm, context_ref),
            *(
                (bev_hbm.at[:, pl.ds(j * LOW, LOW)], bev_ref.at[pl.ds(j * channels, channels), :])
                for j in range(blocks)
            ),
        ])
    ]
    for copy in copies:
        copy.start()
    for copy in copies:
        copy.wait()
    tile = tile_ref[0]
    slot = lax.broadcasted_iota(jnp.int32, (1, capacity), 1)
    ids, ids32 = as_index(row_ids(HALF)), row_ids(LANES)
    ones = jnp.ones((1, capacity), BF16)
    high, low = (half.T for half in halves(probs_ref[...]))
    pad = jnp.zeros((LANES - depth_bins, 2 * pixels), BF16)
    context = context_ref[...].T
    table = jnp.concatenate(
        [
            jnp.concatenate([high, low], axis=1),
            pad,
            jnp.concatenate([context, jnp.zeros_like(context)], axis=1),
        ],
        axis=0,
    )
    for s in range(sources):
        hot, block = lookup_tables(ids, ones, cells_ref[pl.ds(s, 1), :], slot < counts_ref[s, tile])
        picked = jnp.dot(bev_ref[...], hot, preferred_element_type=F32)
        found = picked[:channels]
        for j in range(1, blocks):
            found = jnp.where(block == j, picked[j * channels : (j + 1) * channels], found)
        found_ref[s] = found.astype(BF16)
        pixel, bins = split_points(points_ref[pl.ds(s, 1), :], depth_bins)
        hot = row_hot(ids[:pixels], as_index(pixel), ones)
        spread = jnp.dot(table, jnp.concatenate([hot, hot], axis=0), preferred_element_type=F32)
        prob_ref[pl.ds(s, 1), :] = by_lanes(
            lambda at: jnp.sum(
                jnp.where(ids32 == bins[:, at], spread[:LANES, at], 0.0), axis=0, keepdims=True
            ),
            capacity,
        )
        ctx_ref[s] = spread[LANES:].astype(BF16)


def front(tile, bev_columns, cells, counts, points, depth_probs, context):
    sources, capacity = cells.shape
    channels, cells_dev = bev_columns.shape
    blocks = cells_dev // LOW
    return pl.pallas_call(
        front_kernel,
        out_shape=[
            jax.ShapeDtypeStruct((sources, channels, capacity), BF16),
            jax.ShapeDtypeStruct((sources, capacity), F32),
            jax.ShapeDtypeStruct((sources, channels, capacity), BF16),
        ],
        in_specs=[SMEM] + [HBM] * 6,
        out_specs=[VMEM] * 3,
        scratch_shapes=[
            pltpu.VMEM((blocks * channels, LOW), BF16),
            pltpu.VMEM(cells.shape, jnp.int32),
            pltpu.SMEM(counts.shape, jnp.int32),
            pltpu.VMEM(points.shape, jnp.int32),
            pltpu.VMEM(depth_probs.shape, F32),
            pltpu.VMEM(context.shape, BF16),
            pltpu.SemaphoreType.DMA((5 + blocks,)),
        ],
        compiler_params=pltpu.CompilerParams(vmem_limit_bytes=40 * 2**20),
        cost_estimate=pl.CostEstimate(flops=8 * 10**9, bytes_accessed=4 * 10**6, transcendentals=0),
        name="front",
    )(tile, *(
        pltpu.with_memory_space_constraint(value, pltpu.HBM)
        for value in (bev_columns, cells, counts, points, depth_probs, context)
    ))


def head_kernel(
    arrived_ref, points_ref, prob_ref, ctx_ref, probs_ref, features_ref, grad_ref, weight_ref
):
    pixels, depth_bins = probs_ref.shape
    sources, channels, capacity = arrived_ref.shape
    ids = as_index(row_ids(LANES))
    ones = jnp.ones((1, capacity), BF16)
    total = jnp.zeros((4 * pixels, LANES + channels), F32)
    for s in range(sources):
        arrived = arrived_ref[s]
        slot_grad = jnp.sum(
            arrived.astype(F32) * ctx_ref[s].astype(F32), axis=0, keepdims=True
        )
        pixel, bins = map(as_index, split_points(points_ref[pl.ds(s, 1), :], depth_bins))
        weights = [*halves(slot_grad), *halves(prob_ref[pl.ds(s, 1), :])]
        left = jnp.concatenate([row_hot(ids[:pixels], pixel, weight) for weight in weights], axis=0)
        right = jnp.concatenate([row_hot(ids, bins, ones), arrived], axis=0)
        total += lax.dot_general(left, right, NT, preferred_element_type=F32)
    grad_depth = (total[:pixels] + total[pixels : 2 * pixels])[:, :depth_bins]
    grad_ctx = (total[2 * pixels : 3 * pixels] + total[3 * pixels :])[:, LANES:]
    probs = probs_ref[...]
    grad_logits = probs * (grad_depth - jnp.sum(probs * grad_depth, axis=-1, keepdims=True))
    head_grad = jnp.concatenate([grad_logits, grad_ctx], axis=-1).astype(BF16)
    grad_ref[...] = head_grad
    weight_ref[...] = lax.dot_general(
        features_ref[...], head_grad, TN, preferred_element_type=F32
    ).astype(BF16)


def head(arrived, points, prob, ctx, depth_probs, features):
    pixels, depth_bins = depth_probs.shape
    channels = arrived.shape[1]
    return pl.pallas_call(
        head_kernel,
        out_shape=[
            jax.ShapeDtypeStruct((pixels, depth_bins + channels), BF16),
            jax.ShapeDtypeStruct((features.shape[1], depth_bins + channels), BF16),
        ],
        in_specs=[VMEM] * 6,
        out_specs=[VMEM] * 2,
        compiler_params=pltpu.CompilerParams(vmem_limit_bytes=40 * 2**20),
        cost_estimate=pl.CostEstimate(flops=4 * 10**9, bytes_accessed=4 * 10**6, transcendentals=0),
        name="head",
    )(arrived, points, prob, ctx, depth_probs, features)


def exchange(value, axis):
    return lax.all_to_all(value, axis, split_axis=0, concat_axis=0, tiled=True)


def sum_over_groups(share):
    dp = ("z", "core")
    count = lax.axis_size(dp)

    def swapped(value, bits):
        return lax.ppermute(value, dp, [(i, i ^ bits) for i in range(count)])

    beside, across = swapped(share, 1), (swapped(share, 2), swapped(share, 3))
    share = (share + beside) + (across[0] + across[1])

    def moved(hop):
        return lax.ppermute(share, dp, [(i, (i + hop) % count) for i in range(count)])

    ahead, behind, across = moved(4), moved(-4), moved(8)
    return (ahead + behind) + (share + across)


def body(features, depth_probs, context, bev_grad, head_weight, slot_cell, slot_point, slot_count):
    tile_axes = ("x", "y")
    tiles = lax.axis_size(tile_axes)
    tile = lax.axis_index(tile_axes).astype(jnp.int32).reshape(1)
    points = slot_point[0, 0]
    found, prob, ctx = front(
        tile, bev_grad[0].T, slot_cell[0, 0], slot_count[0], points, depth_probs[0], context[0]
    )
    arrived = exchange(found, tile_axes)
    head_grad, weight_grad = head(arrived, points, prob, ctx, depth_probs[0], features[0])
    rows = weight_grad.shape[0] // tiles
    parts = exchange(weight_grad.reshape(tiles, rows, -1), tile_axes)
    share = parts.astype(F32).sum(axis=0)
    grad_feats = jnp.dot(head_grad, head_weight, preferred_element_type=F32).astype(BF16)
    return (grad_feats[None], sum_over_groups(share))


def solution(mesh):
    dp, tile = ("z", "core"), ("x", "y")
    fine = Mesh(mesh.devices.reshape(8, 2, 4, 4), dp + tile)
    return jax.shard_map(
        body,
        mesh=fine,
        in_specs=(
            P(dp, tile, None),
            P(dp, tile, None),
            P(dp, tile, None),
            P(dp, tile, None),
            P(),
            P(dp, tile, None, None),
            P(dp, tile, None, None),
            P(dp, None, None),
        ),
        out_specs=(P(dp, tile, None), P(tile, None)),
        check_vma=False,
    )
```

```python
import jax
import jax.numpy as jnp
from jax import lax
from jax.experimental import pallas as pl
from jax.experimental.pallas import tpu as pltpu
from jax.sharding import Mesh, PartitionSpec as P

F32, BF16 = jnp.float32, jnp.bfloat16
LOW = 256
LANES = 128
HALF = 256
NT = (((1,), (1,)), ((), ()))
TN = (((0,), (0,)), ((), ()))
VMEM = pl.BlockSpec(memory_space=pltpu.VMEM)
SMEM = pl.BlockSpec(memory_space=pltpu.SMEM)
HBM = pl.BlockSpec(memory_space=pltpu.HBM)


def row_ids(rows):
    return lax.broadcasted_iota(jnp.int32, (rows, LANES), 0)


def as_index(value):
    return value.astype(F32).astype(BF16)


def by_lanes(make, columns):
    return jnp.concatenate([make(slice(i, i + LANES)) for i in range(0, columns, LANES)], axis=1)


def row_hot(ids, index_row, value_row):
    zero = jnp.zeros((), value_row.dtype)
    return by_lanes(
        lambda at: jnp.where(ids == index_row[:, at], value_row[:, at], zero), index_row.shape[1]
    )


def halves(value):
    high = value.astype(BF16)
    return high, (value - high.astype(F32)).astype(BF16)


def split_points(points, depth_bins):
    pixel = (points.astype(F32) + 0.5) * (1.0 / depth_bins)
    pixel = pixel.astype(jnp.int32)
    return pixel, points - pixel * depth_bins


def lookup_tables(ids, ones, cell, live):
    low = cell & (HALF - 1)
    hots = []
    for h in range(LOW // HALF):
        here = live & (((cell >> 8) & (LOW // HALF - 1)) == h)
        hots.append(row_hot(ids, as_index(jnp.where(here, low, -1)), ones))
    return jnp.concatenate(hots, axis=0), cell >> (LOW.bit_length() - 1)


def front_kernel(
    tile_ref, bev_hbm, cells_hbm, counts_hbm, points_hbm, probs_hbm, context_hbm,
    found_ref, prob_ref, ctx_ref,
    bev_ref, cells_ref, counts_ref, points_ref, probs_ref, context_ref, sems,
):
    channels = context_ref.shape[1]
    blocks = bev_ref.shape[1] // LOW
    sources, capacity = cells_ref.shape
    pixels, depth_bins = probs_ref.shape
    copies = [
        pltpu.make_async_copy(source, target, sems.at[i])
        for i, (source, target) in enumerate([
            (bev_hbm, bev_ref),
            (counts_hbm, counts_ref),
            (cells_hbm, cells_ref),
            (points_hbm, points_ref),
            (probs_hbm, probs_ref),
            (context_hbm, context_ref),
        ])
    ]
    for copy in copies:
        copy.start()
    for copy in copies:
        copy.wait()
    tile = tile_ref[0]
    slot = lax.broadcasted_iota(jnp.int32, (1, capacity), 1)
    ids, ids32 = as_index(row_ids(HALF)), row_ids(LANES)
    ones = jnp.ones((1, capacity), BF16)
    high, low = (half.T for half in halves(probs_ref[...]))
    pad = jnp.zeros((LANES - depth_bins, 2 * pixels), BF16)
    context = context_ref[...].T
    table = jnp.concatenate(
        [
            jnp.concatenate([high, low], axis=1),
            pad,
            jnp.concatenate([context, jnp.zeros_like(context)], axis=1),
        ],
        axis=0,
    )
    grid = jnp.concatenate([bev_ref[:, pl.ds(j * LOW, LOW)] for j in range(blocks)], axis=0)
    for s in range(sources):
        hot, block = lookup_tables(ids, ones, cells_ref[pl.ds(s, 1), :], slot < counts_ref[s, tile])
        picked = jnp.dot(grid, hot, preferred_element_type=F32)
        found = picked[:channels]
        for j in range(1, blocks):
            found = jnp.where(block == j, picked[j * channels : (j + 1) * channels], found)
        found_ref[s] = found.astype(BF16)
        pixel, bins = split_points(points_ref[pl.ds(s, 1), :], depth_bins)
        hot = row_hot(ids[:pixels], as_index(pixel), ones)
        spread = jnp.dot(table, jnp.concatenate([hot, hot], axis=0), preferred_element_type=F32)
        prob_ref[pl.ds(s, 1), :] = by_lanes(
            lambda at: jnp.sum(
                jnp.where(ids32 == bins[:, at], spread[:LANES, at], 0.0), axis=0, keepdims=True
            ),
            capacity,
        )
        ctx_ref[s] = spread[LANES:].astype(BF16)


def front(tile, bev_columns, cells, counts, points, depth_probs, context):
    sources, capacity = cells.shape
    channels = bev_columns.shape[0]
    return pl.pallas_call(
        front_kernel,
        out_shape=[
            jax.ShapeDtypeStruct((sources, channels, capacity), BF16),
            jax.ShapeDtypeStruct((sources, capacity), F32),
            jax.ShapeDtypeStruct((sources, channels, capacity), BF16),
        ],
        in_specs=[SMEM] + [HBM] * 6,
        out_specs=[VMEM] * 3,
        scratch_shapes=[
            pltpu.VMEM(bev_columns.shape, BF16),
            pltpu.VMEM(cells.shape, jnp.int32),
            pltpu.SMEM(counts.shape, jnp.int32),
            pltpu.VMEM(points.shape, jnp.int32),
            pltpu.VMEM(depth_probs.shape, F32),
            pltpu.VMEM(context.shape, BF16),
            pltpu.SemaphoreType.DMA((6,)),
        ],
        compiler_params=pltpu.CompilerParams(vmem_limit_bytes=40 * 2**20),
        cost_estimate=pl.CostEstimate(flops=8 * 10**9, bytes_accessed=4 * 10**6, transcendentals=0),
        name="front",
    )(tile, *(
        pltpu.with_memory_space_constraint(value, pltpu.HBM)
        for value in (bev_columns, cells, counts, points, depth_probs, context)
    ))


def head_kernel(
    arrived_ref, points_ref, prob_ref, ctx_ref, probs_ref, features_ref, grad_ref, weight_ref
):
    pixels, depth_bins = probs_ref.shape
    sources, channels, capacity = arrived_ref.shape
    ids = as_index(row_ids(LANES))
    ones = jnp.ones((1, capacity), BF16)
    total = jnp.zeros((4 * pixels, LANES + channels), F32)
    for s in range(sources):
        arrived = arrived_ref[s]
        slot_grad = jnp.sum(
            arrived.astype(F32) * ctx_ref[s].astype(F32), axis=0, keepdims=True
        )
        pixel, bins = map(as_index, split_points(points_ref[pl.ds(s, 1), :], depth_bins))
        weights = [*halves(slot_grad), *halves(prob_ref[pl.ds(s, 1), :])]
        left = jnp.concatenate([row_hot(ids[:pixels], pixel, weight) for weight in weights], axis=0)
        right = jnp.concatenate([row_hot(ids, bins, ones), arrived], axis=0)
        total += lax.dot_general(left, right, NT, preferred_element_type=F32)
    grad_depth = (total[:pixels] + total[pixels : 2 * pixels])[:, :depth_bins]
    grad_ctx = (total[2 * pixels : 3 * pixels] + total[3 * pixels :])[:, LANES:]
    probs = probs_ref[...]
    grad_logits = probs * (grad_depth - jnp.sum(probs * grad_depth, axis=-1, keepdims=True))
    head_grad = jnp.concatenate([grad_logits, grad_ctx], axis=-1).astype(BF16)
    grad_ref[...] = head_grad
    weight_ref[...] = lax.dot_general(
        features_ref[...], head_grad, TN, preferred_element_type=F32
    ).astype(BF16)


def head(arrived, points, prob, ctx, depth_probs, features):
    pixels, depth_bins = depth_probs.shape
    channels = arrived.shape[1]
    return pl.pallas_call(
        head_kernel,
        out_shape=[
            jax.ShapeDtypeStruct((pixels, depth_bins + channels), BF16),
            jax.ShapeDtypeStruct((features.shape[1], depth_bins + channels), BF16),
        ],
        in_specs=[VMEM] * 6,
        out_specs=[VMEM] * 2,
        compiler_params=pltpu.CompilerParams(vmem_limit_bytes=40 * 2**20),
        cost_estimate=pl.CostEstimate(flops=4 * 10**9, bytes_accessed=4 * 10**6, transcendentals=0),
        name="head",
    )(arrived, points, prob, ctx, depth_probs, features)


def exchange(value, axis):
    return lax.all_to_all(value, axis, split_axis=0, concat_axis=0, tiled=True)


def sum_over_groups(share):
    dp = ("z", "core")
    count = lax.axis_size(dp)

    def swapped(value, bits):
        return lax.ppermute(value, dp, [(i, i ^ bits) for i in range(count)])

    beside, across = swapped(share, 1), (swapped(share, 2), swapped(share, 3))
    share = (share + beside) + (across[0] + across[1])
    two, four, six = (swapped(share, 2 * chips) for chips in (2, 4, 6))
    return (two + six) + (share + four)


def body(features, depth_probs, context, bev_grad, head_weight, slot_cell, slot_point, slot_count):
    tile_axes = ("x", "y")
    tiles = lax.axis_size(tile_axes)
    tile = lax.axis_index(tile_axes).astype(jnp.int32).reshape(1)
    points = slot_point[0, 0]
    found, prob, ctx = front(
        tile, bev_grad[0].T, slot_cell[0, 0], slot_count[0], points, depth_probs[0], context[0]
    )
    arrived = exchange(found, tile_axes)
    head_grad, weight_grad = head(arrived, points, prob, ctx, depth_probs[0], features[0])
    rows = weight_grad.shape[0] // tiles
    parts = exchange(weight_grad.reshape(tiles, rows, -1), tile_axes)
    share = parts.astype(F32).sum(axis=0)
    grad_feats = jnp.dot(head_grad, head_weight, preferred_element_type=F32).astype(BF16)
    return (grad_feats[None], sum_over_groups(share))


def solution(mesh):
    dp, tile = ("z", "core"), ("x", "y")
    fine = Mesh(mesh.devices.reshape(8, 2, 4, 4), dp + tile)
    return jax.shard_map(
        body,
        mesh=fine,
        in_specs=(
            P(dp, tile, None),
            P(dp, tile, None),
            P(dp, tile, None),
            P(dp, tile, None),
            P(),
            P(dp, tile, None, None),
            P(dp, tile, None, None),
            P(dp, None, None),
        ),
        out_specs=(P(dp, tile, None), P(tile, None)),
        check_vma=False,
    )
```

```python
import jax
import jax.numpy as jnp
from jax import lax
from jax.experimental import pallas as pl
from jax.experimental.pallas import tpu as pltpu
from jax.sharding import Mesh, PartitionSpec as P

F32, BF16 = jnp.float32, jnp.bfloat16
LOW = 512
LANES = 128
HALF = 256
NT = (((1,), (1,)), ((), ()))
TN = (((0,), (0,)), ((), ()))
VMEM = pl.BlockSpec(memory_space=pltpu.VMEM)
SMEM = pl.BlockSpec(memory_space=pltpu.SMEM)
HBM = pl.BlockSpec(memory_space=pltpu.HBM)


def row_ids(rows):
    return lax.broadcasted_iota(jnp.int32, (rows, LANES), 0)


def as_index(value):
    return value.astype(F32).astype(BF16)


def by_lanes(make, columns):
    return jnp.concatenate([make(slice(i, i + LANES)) for i in range(0, columns, LANES)], axis=1)


def row_hot(ids, index_row, value_row):
    zero = jnp.zeros((), value_row.dtype)
    return by_lanes(
        lambda at: jnp.where(ids == index_row[:, at], value_row[:, at], zero), index_row.shape[1]
    )


def halves(value):
    high = value.astype(BF16)
    return high, (value - high.astype(F32)).astype(BF16)


def split_points(points, depth_bins):
    pixel = (points.astype(F32) + 0.5) * (1.0 / depth_bins)
    pixel = pixel.astype(jnp.int32)
    return pixel, points - pixel * depth_bins


def lookup_tables(ids, ones, cell, live):
    low = cell & (HALF - 1)
    hots = []
    for h in range(LOW // HALF):
        here = live & (((cell >> 8) & (LOW // HALF - 1)) == h)
        hots.append(row_hot(ids, as_index(jnp.where(here, low, -1)), ones))
    return jnp.concatenate(hots, axis=0), cell >> (LOW.bit_length() - 1)


def front_kernel(
    tile_ref, bev_hbm, cells_hbm, counts_hbm, points_hbm, probs_hbm, context_hbm,
    found_ref, prob_ref, ctx_ref,
    bev_ref, cells_ref, counts_ref, points_ref, probs_ref, context_ref, sems,
):
    channels = context_ref.shape[1]
    blocks = bev_ref.shape[0] // channels
    sources, capacity = cells_ref.shape
    pixels, depth_bins = probs_ref.shape
    copies = [
        pltpu.make_async_copy(source, target, sems.at[i])
        for i, (source, target) in enumerate([
            (counts_hbm, counts_ref),
            (cells_hbm, cells_ref),
            (points_hbm, points_ref),
            (probs_hbm, probs_ref),
            (context_hbm, context_ref),
            *(
                (bev_hbm.at[:, pl.ds(j * LOW, LOW)], bev_ref.at[pl.ds(j * channels, channels), :])
                for j in range(blocks)
            ),
        ])
    ]
    for copy in copies:
        copy.start()
    for copy in copies:
        copy.wait()
    tile = tile_ref[0]
    slot = lax.broadcasted_iota(jnp.int32, (1, capacity), 1)
    ids, ids32 = as_index(row_ids(HALF)), row_ids(LANES)
    ones = jnp.ones((1, capacity), BF16)
    high, low = (half.T for half in halves(probs_ref[...]))
    pad = jnp.zeros((LANES - depth_bins, 2 * pixels), BF16)
    context = context_ref[...].T
    table = jnp.concatenate(
        [
            jnp.concatenate([high, low], axis=1),
            pad,
            jnp.concatenate([context, jnp.zeros_like(context)], axis=1),
        ],
        axis=0,
    )
    for s in range(sources):
        hot, block = lookup_tables(ids, ones, cells_ref[pl.ds(s, 1), :], slot < counts_ref[s, tile])
        picked = jnp.dot(bev_ref[...], hot, preferred_element_type=F32)
        found = picked[:channels]
        for j in range(1, blocks):
            found = jnp.where(block == j, picked[j * channels : (j + 1) * channels], found)
        found_ref[s] = found.astype(BF16)
        pixel, bins = split_points(points_ref[pl.ds(s, 1), :], depth_bins)
        hot = row_hot(ids[:pixels], as_index(pixel), ones)
        spread = jnp.dot(table, jnp.concatenate([hot, hot], axis=0), preferred_element_type=F32)
        prob_ref[pl.ds(s, 1), :] = by_lanes(
            lambda at: jnp.sum(
                jnp.where(ids32 == bins[:, at], spread[:LANES, at], 0.0), axis=0, keepdims=True
            ),
            capacity,
        )
        ctx_ref[s] = spread[LANES:].astype(BF16)


def front(tile, bev_columns, cells, counts, points, depth_probs, context):
    sources, capacity = cells.shape
    channels, cells_dev = bev_columns.shape
    blocks = cells_dev // LOW
    return pl.pallas_call(
        front_kernel,
        out_shape=[
            jax.ShapeDtypeStruct((sources, channels, capacity), BF16),
            jax.ShapeDtypeStruct((sources, capacity), F32),
            jax.ShapeDtypeStruct((sources, channels, capacity), BF16),
        ],
        in_specs=[SMEM] + [HBM] * 6,
        out_specs=[VMEM] * 3,
        scratch_shapes=[
            pltpu.VMEM((blocks * channels, LOW), BF16),
            pltpu.VMEM(cells.shape, jnp.int32),
            pltpu.SMEM(counts.shape, jnp.int32),
            pltpu.VMEM(points.shape, jnp.int32),
            pltpu.VMEM(depth_probs.shape, F32),
            pltpu.VMEM(context.shape, BF16),
            pltpu.SemaphoreType.DMA((5 + blocks,)),
        ],
        compiler_params=pltpu.CompilerParams(vmem_limit_bytes=40 * 2**20),
        cost_estimate=pl.CostEstimate(flops=8 * 10**9, bytes_accessed=4 * 10**6, transcendentals=0),
        name="front",
    )(tile, *(
        pltpu.with_memory_space_constraint(value, pltpu.HBM)
        for value in (bev_columns, cells, counts, points, depth_probs, context)
    ))


def head_kernel(
    arrived_ref, points_ref, prob_ref, ctx_ref, probs_ref, features_ref, grad_ref, weight_ref
):
    pixels, depth_bins = probs_ref.shape
    sources, channels, capacity = arrived_ref.shape
    ids = as_index(row_ids(LANES))
    ones = jnp.ones((1, capacity), BF16)
    total = jnp.zeros((4 * pixels, LANES + channels), F32)
    for s in range(sources):
        arrived = arrived_ref[s]
        slot_grad = jnp.sum(
            arrived.astype(F32) * ctx_ref[s].astype(F32), axis=0, keepdims=True
        )
        pixel, bins = map(as_index, split_points(points_ref[pl.ds(s, 1), :], depth_bins))
        weights = [*halves(slot_grad), *halves(prob_ref[pl.ds(s, 1), :])]
        left = jnp.concatenate([row_hot(ids[:pixels], pixel, weight) for weight in weights], axis=0)
        right = jnp.concatenate([row_hot(ids, bins, ones), arrived], axis=0)
        total += lax.dot_general(left, right, NT, preferred_element_type=F32)
    grad_depth = (total[:pixels] + total[pixels : 2 * pixels])[:, :depth_bins]
    grad_ctx = (total[2 * pixels : 3 * pixels] + total[3 * pixels :])[:, LANES:]
    probs = probs_ref[...]
    grad_logits = probs * (grad_depth - jnp.sum(probs * grad_depth, axis=-1, keepdims=True))
    head_grad = jnp.concatenate([grad_logits, grad_ctx], axis=-1).astype(BF16)
    grad_ref[...] = head_grad
    weight_ref[...] = lax.dot_general(
        features_ref[...], head_grad, TN, preferred_element_type=F32
    ).astype(BF16)


def head(arrived, points, prob, ctx, depth_probs, features):
    pixels, depth_bins = depth_probs.shape
    channels = arrived.shape[1]
    return pl.pallas_call(
        head_kernel,
        out_shape=[
            jax.ShapeDtypeStruct((pixels, depth_bins + channels), BF16),
            jax.ShapeDtypeStruct((features.shape[1], depth_bins + channels), BF16),
        ],
        in_specs=[VMEM] * 6,
        out_specs=[VMEM] * 2,
        compiler_params=pltpu.CompilerParams(vmem_limit_bytes=40 * 2**20),
        cost_estimate=pl.CostEstimate(flops=4 * 10**9, bytes_accessed=4 * 10**6, transcendentals=0),
        name="head",
    )(arrived, points, prob, ctx, depth_probs, features)


def exchange(value, axis):
    return lax.all_to_all(value, axis, split_axis=0, concat_axis=0, tiled=True)


def sum_over_groups(share, also):
    dp = ("z", "core")
    count = lax.axis_size(dp)

    def swapped(value, bits):
        return lax.ppermute(value, dp, [(i, i ^ bits) for i in range(count)])

    beside, across = swapped(share, 1), (swapped(share, 2), swapped(share, 3))
    share = (share + beside) + (across[0] + across[1])
    share, also = lax.optimization_barrier((share, also))

    def moved(hop):
        return lax.ppermute(share, dp, [(i, (i + hop) % count) for i in range(count)])

    ahead, behind, across = moved(4), moved(-4), moved(8)
    return (ahead + behind) + (share + across), also


def body(features, depth_probs, context, bev_grad, head_weight, slot_cell, slot_point, slot_count):
    tile_axes = ("x", "y")
    tiles = lax.axis_size(tile_axes)
    tile = lax.axis_index(tile_axes).astype(jnp.int32).reshape(1)
    points = slot_point[0, 0]
    found, prob, ctx = front(
        tile, bev_grad[0].T, slot_cell[0, 0], slot_count[0], points, depth_probs[0], context[0]
    )
    arrived = exchange(found, tile_axes)
    head_grad, weight_grad = head(arrived, points, prob, ctx, depth_probs[0], features[0])
    rows = weight_grad.shape[0] // tiles
    parts = exchange(weight_grad.reshape(tiles, rows, -1), tile_axes)
    share = parts.astype(F32).sum(axis=0)
    grad_feats = jnp.dot(head_grad, head_weight, preferred_element_type=F32).astype(BF16)
    summed, grad_feats = sum_over_groups(share, grad_feats)
    return (grad_feats[None], summed)


def solution(mesh):
    dp, tile = ("z", "core"), ("x", "y")
    fine = Mesh(mesh.devices.reshape(8, 2, 4, 4), dp + tile)
    return jax.shard_map(
        body,
        mesh=fine,
        in_specs=(
            P(dp, tile, None),
            P(dp, tile, None),
            P(dp, tile, None),
            P(dp, tile, None),
            P(),
            P(dp, tile, None, None),
            P(dp, tile, None, None),
            P(dp, None, None),
        ),
        out_specs=(P(dp, tile, None), P(tile, None)),
        check_vma=False,
    )
```
